32 devices in a mesh: seq: 8 (over z, x), dp: 4 (over y, core).
Axes of the slice: x: 2, y: 2, z: 4, core: 2. Of those that a mesh axis runs over, the one named last changes fastest.
Arguments:
- query: bfloat16 [4, 4096, 2048], P('dp', 'seq'), may hold values from -100 to 100
- key: bfloat16 [4, 4096, 2048], P('dp', 'seq'), may hold values from -6 to 6
- value: bfloat16 [4, 4096, 2048], P('dp', 'seq'), may hold values from -6 to 6
- grad_ctx: bfloat16 [4, 4096, 2048], P('dp', 'seq'), may hold values from -6 to 6
- proj_key: bfloat16 [512, 4096], P(None, 'seq'), may hold values from -0.09375 to 0.09375
- proj_value: bfloat16 [512, 4096], P(None, 'seq'), may hold values from -0.09375 to 0.09375
Outputs:
- grad_query: bfloat16 [4, 4096, 2048], P('dp', 'seq')
- grad_key: bfloat16 [4, 4096, 2048], P('dp', 'seq')
- grad_value: bfloat16 [4, 4096, 2048], P('dp', 'seq')
- grad_proj_key: bfloat16 [512, 4096], P('dp', 'seq')
- grad_proj_value: bfloat16 [512, 4096], P('dp', 'seq')
The draws below stay inside these ranges and needn't reach their ends.
All inputs are finite; a program needn't handle non-finite values.
Results may differ from the reference program's by a relative error of at most 0.034.
The reference program's roundings to bfloat16 on the way count: a program that leaves them out, or rounds other values in their place, can miss the bound.
Values may be sent and summed in bfloat16 or wider, within the bound.
A program may use at most 128 MiB of HBM per device.

```python
import jax
import jax.numpy as jnp
from jax import lax

H = 16
HEAD_DIM = 128
KP = 512
HD = 2048
SEQ_LEN = 4096
N_DP = 4


def draw_query(key, part):
    key = jax.random.fold_in(key, 5)
    first = jax.random.fold_in(key, 0)
    shape = (N_DP, SEQ_LEN, HD)
    values = jnp.clip(jax.random.normal(first, shape, jnp.float32), -5.0, 5.0)
    return values.astype(jnp.bfloat16)


def shard_levels(rng, extent, shards, least, top_value):
    def one(axis_at, parts):
        steps = jax.random.uniform(jax.random.fold_in(jax.random.fold_in(rng, 6), axis_at), (parts,), jnp.float32, least / len(shards), top_value / len(shards))
        return jnp.repeat(jnp.exp(steps), extent[axis_at] // parts).reshape((-1,) + (1,) * (len(extent) - axis_at - 1))

    factor_of = one(*shards[0])
    for cut in shards[1:]:
        factor_of = factor_of * one(*cut)
    return factor_of


def noise(rng, extent, width, reach, cuts=(), dtype=jnp.bfloat16):
    level = shard_levels(rng, extent, cuts, -0.22, 0.18) if cuts else 1.0
    result = jax.random.normal(rng, extent, jnp.float32) * width * level
    return jnp.minimum(jnp.maximum(result, -reach), reach).astype(dtype)


def setup_inputs(seed: int = 0) -> dict:
    key_list = jax.random.split(jax.random.key(seed), 7)
    return {
        "query": draw_query(jax.random.fold_in(key_list[6], 71), 0),
        "key": noise(key_list[1], (N_DP, SEQ_LEN, HD), 1.0, 6.0, ((0, 4), (1, 8))),
        "value": noise(key_list[2], (N_DP, SEQ_LEN, HD), 1.0, 6.0, ((0, 4), (1, 8))),
        "grad_ctx": noise(key_list[3], (N_DP, SEQ_LEN, HD), 1.0, 6.0, ((0, 4), (1, 8))),
        "proj_key": noise(key_list[4], (KP, SEQ_LEN), SEQ_LEN ** -0.5, 0.09375, ((1, 8),)),
        "proj_value": noise(key_list[5], (KP, SEQ_LEN), SEQ_LEN ** -0.5, 0.09375, ((1, 8),)),
    }


def head_pass(q, g, kp, vp):
    scale = HEAD_DIM ** -0.5
    hd_total = q.shape[1]
    rows = q.shape[0]
    gq = jnp.zeros((rows, hd_total), jnp.bfloat16)
    dkp = jnp.zeros((kp.shape[0], hd_total), jnp.float32)
    dvp = jnp.zeros((kp.shape[0], hd_total), jnp.float32)

    def per_head(h, carry):
        gq, dkp, dvp = carry
        start = (h * HEAD_DIM).astype(jnp.int32)
        q_head = lax.dynamic_slice_in_dim(q, start, HEAD_DIM, 1)
        g_head = lax.dynamic_slice_in_dim(g, start, HEAD_DIM, 1)
        kp_head = lax.dynamic_slice_in_dim(kp, start, HEAD_DIM, 1)
        vp_head = lax.dynamic_slice_in_dim(vp, start, HEAD_DIM, 1)
        scores = lax.dot_general(q_head, kp_head, (((1,), (1,)), ((), ())), preferred_element_type=jnp.float32) * scale
        probs = jax.nn.softmax(scores, axis=-1)
        probs_low = probs.astype(jnp.bfloat16)
        grad_probs = lax.dot_general(g_head, vp_head, (((1,), (1,)), ((), ())), preferred_element_type=jnp.float32)
        delta = jnp.sum(probs * grad_probs, axis=-1, keepdims=True)
        grad_scores = (probs * (grad_probs - delta) * scale).astype(jnp.bfloat16)
        gq_head = jnp.dot(grad_scores, kp_head, preferred_element_type=jnp.float32).astype(jnp.bfloat16)
        dkp_head = lax.dot_general(grad_scores, q_head, (((0,), (0,)), ((), ())), preferred_element_type=jnp.float32)
        dvp_head = lax.dot_general(probs_low, g_head, (((0,), (0,)), ((), ())), preferred_element_type=jnp.float32)
        gq = lax.dynamic_update_slice_in_dim(gq, gq_head, start, 1)
        dkp = lax.dynamic_update_slice_in_dim(dkp, dkp_head, start, 1)
        dvp = lax.dynamic_update_slice_in_dim(dvp, dvp_head, start, 1)
        return gq, dkp, dvp

    return lax.fori_loop(0, H, per_head, (gq, dkp, dvp))


def reference(query, key, value, grad_ctx, proj_key, proj_value):
    gq_all = []
    gk_all = []
    gv_all = []
    sum_pk = jnp.zeros((KP, SEQ_LEN), jnp.float32)
    sum_pv = jnp.zeros((KP, SEQ_LEN), jnp.float32)
    for rep in range(N_DP):
        q = query[rep]
        k = key[rep]
        v = value[rep]
        g = grad_ctx[rep]
        kp = jnp.dot(proj_key, k, preferred_element_type=jnp.float32).astype(jnp.bfloat16)
        vp = jnp.dot(proj_value, v, preferred_element_type=jnp.float32).astype(jnp.bfloat16)
        gq, dkp, dvp = head_pass(q, g, kp, vp)
        dkp = dkp.astype(jnp.bfloat16)
        dvp = dvp.astype(jnp.bfloat16)
        gk = lax.dot_general(proj_key, dkp, (((0,), (0,)), ((), ())), preferred_element_type=jnp.float32).astype(jnp.bfloat16)
        gv = lax.dot_general(proj_value, dvp, (((0,), (0,)), ((), ())), preferred_element_type=jnp.float32).astype(jnp.bfloat16)
        sum_pk = sum_pk + lax.dot_general(dkp, k, (((1,), (1,)), ((), ())), preferred_element_type=jnp.float32)
        sum_pv = sum_pv + lax.dot_general(dvp, v, (((1,), (1,)), ((), ())), preferred_element_type=jnp.float32)
        gq_all.append(gq)
        gk_all.append(gk)
        gv_all.append(gv)
    return (jnp.stack(gq_all), jnp.stack(gk_all), jnp.stack(gv_all), sum_pk.astype(jnp.bfloat16), sum_pv.astype(jnp.bfloat16))
```

```python
import functools

import jax
import jax.numpy as jnp
from jax import lax
from jax.experimental import pallas as pl
from jax.experimental.pallas import tpu as pltpu
from jax.sharding import PartitionSpec as P

HEAD_DIM = 128
INNER = 2
RECV = 8
SLOTS = 4
A, B, C, D, E, F, G, Z, I = 0, 2, 3, 4, 5, 7, 8, 9, 10
NT = (((1,), (1,)), ((), ()))


def dot(a, b):
    return jnp.dot(a, b, preferred_element_type=jnp.float32)


def dot_nt(a, b):
    return lax.dot_general(a, b, NT, preferred_element_type=jnp.float32)


def kernel(
    n_seq, n_dp,
    q_ref, k_ref, v_ref, g_ref, pk_ref, pv_ref, pkt_ref, pvt_ref,
    gq_ref, gk_ref, gv_ref, sk_ref, sv_ref,
    own_k, own_v, snd_k, snd_v, half_v, arr_k, arr_v, blk_k, blk_v, full,
    own_d, snd_d, half_d, arr_d, blk_d, full_d,
    term, snd_t, arr_t,
    s_pair, r_pair, s_grp, r_grp, s_dp, r_dp,
):
    kp_rows = pk_ref.shape[0]
    n_chunks = q_ref.shape[1] // HEAD_DIM
    n_out = n_seq // INNER
    half = kp_rows // INNER
    blk = half // n_out
    t_rows = kp_rows // n_dp
    scale = HEAD_DIM ** (-0.5)
    bf = jnp.bfloat16

    seq = lax.axis_index("seq")
    dp = lax.axis_index("dp")
    x = lax.rem(seq, INNER)
    z = seq // INNER
    mate = seq + 1 - 2 * x
    mine = pl.multiple_of(x * half, half)
    other = pl.multiple_of((1 - x) * half, half)

    def z_at(j):
        return lax.rem(z + j, n_out)

    def peer(j):
        return z_at(j) * INNER + x

    barrier = pltpu.get_barrier_semaphore()
    pl.semaphore_signal(barrier, inc=1, device_id={"seq": mate})
    for j in range(1, n_out):
        pl.semaphore_signal(barrier, inc=1, device_id={"seq": peer(j)})
    for j in range(1, n_dp):
        pl.semaphore_signal(barrier, inc=1, device_id={"dp": lax.rem(dp + j, n_dp)})
    pl.semaphore_wait(barrier, 1 + (n_out - 1) + (n_dp - 1))

    def cols(c):
        return pl.ds(pl.multiple_of(c * HEAD_DIM, HEAD_DIM), HEAD_DIM)

    def pair_copy(kind, src, dst, c):
        return pltpu.make_async_remote_copy(
            src_ref=src, dst_ref=dst,
            send_sem=s_pair.at[kind, lax.rem(c, SLOTS)],
            recv_sem=r_pair.at[kind, lax.rem(c, RECV)],
            device_id={"seq": mate},
        )

    def grp_copy(kind, j, src, dst, c):
        return pltpu.make_async_remote_copy(
            src_ref=src, dst_ref=dst,
            send_sem=s_grp.at[kind, j - 1, lax.rem(c, SLOTS)],
            recv_sem=r_grp.at[kind, j - 1, lax.rem(c, RECV)],
            device_id={"seq": peer(j)},
        )

    def a_copies(c):
        s = lax.rem(c, SLOTS)
        return [
            pair_copy(0, snd_k.at[s], arr_k.at[c], c),
            pair_copy(1, snd_v.at[s], arr_v.at[c], c),
        ]

    def b_copies(c):
        s = lax.rem(c, SLOTS)
        out = []
        for j in range(1, n_out):
            rows = pl.ds(pl.multiple_of(z_at(j) * blk, blk), blk)
            out.append(grp_copy(0, j, own_k.at[s, rows], blk_k.at[c, j - 1], c))
            out.append(grp_copy(1, j, half_v.at[s, rows], blk_v.at[c, j - 1], c))
        return out

    own_rows = pl.ds(pl.multiple_of(x * half + z * blk, blk), blk)
    half_rows = pl.ds(mine, half)
    in_half = pl.ds(pl.multiple_of(z * blk, blk), blk)

    def gather_copies(kind, buf, c):
        ref = buf.at[c, :, own_rows]
        return [grp_copy(kind, j, ref, ref, c) for j in range(1, n_out)]

    def mate_copies(kind, buf, c):
        ref = buf.at[c, :, half_rows]
        return [pair_copy(kind, ref, ref, c)]

    def e_copies(c):
        return [pair_copy(3, snd_d.at[lax.rem(c, SLOTS)], arr_d.at[c], c)]

    def f_copies(c):
        s = lax.rem(c, SLOTS)
        out = []
        for j in range(1, n_out):
            rows = pl.ds(pl.multiple_of(z_at(j) * blk, blk), blk)
            out.append(grp_copy(3, j, half_d.at[s, :, rows], blk_d.at[c, j - 1], c))
        return out

    def start(copies):
        for copy in copies:
            copy.start()

    def wait(copies):
        for copy in copies:
            copy.wait()

    def stage_a(c):
        s = lax.rem(c, SLOTS)
        kc = k_ref[:, cols(c)]
        vc = v_ref[:, cols(c)]
        snd_k[s] = dot(pk_ref[pl.ds(other, half), :], kc)
        snd_v[s] = dot(pv_ref[pl.ds(other, half), :], vc).astype(bf)
        start(a_copies(c))
        own_k[s] = dot(pk_ref[pl.ds(mine, half), :], kc)
        own_v[s] = dot(pv_ref[pl.ds(mine, half), :], vc)

    def stage_b(c):
        s = lax.rem(c, SLOTS)
        wait(a_copies(c))
        own_k[s] = own_k[s] + arr_k[c]
        both = own_v[s] + arr_v[c].astype(jnp.float32)
        own_v[s] = both
        half_v[s] = both.astype(bf)
        start(b_copies(c))

    def stage_c(c):
        s = lax.rem(c, SLOTS)
        wait(b_copies(c))
        kt = own_k[s, in_half]
        vt = own_v[s, in_half]
        for j in range(1, n_out):
            kt += blk_k[c, j - 1]
            vt += blk_v[c, j - 1].astype(jnp.float32)
        full[c, 0, own_rows] = kt.astype(bf)
        full[c, 1, own_rows] = vt.astype(bf)
        start(gather_copies(2, full, c))

    def stage_d(c):
        wait(gather_copies(2, full, c))
        start(mate_copies(2, full, c))

    def stage_e(c):
        s = lax.rem(c, SLOTS)
        wait(mate_copies(2, full, c))
        kp = full[c, 0]
        vp = full[c, 1]
        kpt = kp.astype(jnp.float32).T.astype(bf)
        n_pos = q_ref.shape[0]
        step = min(256, n_pos)
        dk = jnp.zeros((kp_rows, HEAD_DIM), jnp.float32)
        dv = jnp.zeros((kp_rows, HEAD_DIM), jnp.float32)
        for p in range(0, n_pos, step):
            qb = q_ref[pl.ds(p, step), cols(c)]
            gb = g_ref[pl.ds(p, step), cols(c)]
            scores = dot_nt(kp, qb) * scale
            e = jnp.exp(scores - jnp.max(scores, axis=0, keepdims=True))
            probs = e * (1.0 / jnp.sum(e, axis=0, keepdims=True))
            dv += dot(probs.astype(bf), gb)
            gp = dot_nt(vp, gb)
            delta = jnp.sum(probs * gp, axis=0, keepdims=True)
            gs = (probs * (gp - delta) * scale).astype(bf)
            dk += dot(gs, qb)
            gq_ref[pl.ds(p, step), cols(c)] = dot(kpt, gs).T.astype(bf)
        own_d[s, 0] = jnp.where(x == 0, dk[:half], dk[half:])
        own_d[s, 1] = jnp.where(x == 0, dv[:half], dv[half:])
        snd_d[s, 0] = jnp.where(x == 0, dk[half:], dk[:half]).astype(bf)
        snd_d[s, 1] = jnp.where(x == 0, dv[half:], dv[:half]).astype(bf)
        start(e_copies(c))

    def stage_f(c):
        s = lax.rem(c, SLOTS)
        wait(e_copies(c))
        both = own_d[s] + arr_d[c].astype(jnp.float32)
        own_d[s] = both
        half_d[s] = both.astype(bf)
        start(f_copies(c))

    def stage_g(c):
        s = lax.rem(c, SLOTS)
        wait(f_copies(c))
        total = own_d[s, :, in_half]
        for j in range(1, n_out):
            total += blk_d[c, j - 1].astype(jnp.float32)
        full_d[c, :, own_rows] = total.astype(bf)
        start(gather_copies(4, full_d, c))

    def stage_z(c):
        wait(gather_copies(4, full_d, c))
        start(mate_copies(4, full_d, c))

    def stage_i(c):
        wait(mate_copies(4, full_d, c))
        dkp = full_d[c, 0]
        dvp = full_d[c, 1]
        gk_ref[:, cols(c)] = dot(pkt_ref[...], dkp).astype(bf)
        gv_ref[:, cols(c)] = dot(pvt_ref[...], dvp).astype(bf)
        term[0] += dot_nt(dkp, k_ref[:, cols(c)])
        term[1] += dot_nt(dvp, v_ref[:, cols(c)])

    term[...] = jnp.zeros_like(term)

    stages = (
        (E, stage_e), (A, stage_a), (D, stage_d), (Z, stage_z), (C, stage_c), (G, stage_g),
        (B, stage_b), (F, stage_f), (I, stage_i),
    )

    def iteration(i, _):
        for at, stage in stages:
            pl.when((i >= at) & (i < at + n_chunks))(functools.partial(stage, i - at))
        return 0

    lax.fori_loop(0, n_chunks + I, iteration, 0)

    snd_t[...] = term[...].astype(bf)
    copies = []
    for j in range(1, n_dp):
        to = lax.rem(dp + j, n_dp)
        rows = pl.ds(pl.multiple_of(to * t_rows, t_rows), t_rows)
        copies.append(
            pltpu.make_async_remote_copy(
                src_ref=snd_t.at[:, rows], dst_ref=arr_t.at[j - 1],
                send_sem=s_dp.at[j - 1], recv_sem=r_dp.at[j - 1],
                device_id={"dp": to},
            )
        )
    start(copies)
    wait(copies)
    total = term[:, pl.ds(pl.multiple_of(dp * t_rows, t_rows), t_rows)]
    for j in range(1, n_dp):
        total += arr_t[j - 1].astype(jnp.float32)
    sk_ref[...] = total[0].astype(bf)
    sv_ref[...] = total[1].astype(bf)


def body(n_seq, n_dp, query, key, value, grad_ctx, proj_key, proj_value):
    _, n_pos, hd = query.shape
    kp_rows = proj_key.shape[0]
    n_chunks = hd // HEAD_DIM
    n_out = n_seq // INNER
    half = kp_rows // INNER
    blk = half // n_out
    t_rows = kp_rows // n_dp
    w = HEAD_DIM
    f32, bf = jnp.float32, jnp.bfloat16
    dma = pltpu.SemaphoreType.DMA
    vmem = pl.BlockSpec(memory_space=pltpu.VMEM)
    wide = jax.ShapeDtypeStruct((n_pos, hd), bf)
    tall = jax.ShapeDtypeStruct((t_rows, n_pos), bf)
    out = pl.pallas_call(
        functools.partial(kernel, n_seq, n_dp),
        out_shape=(wide, wide, wide, tall, tall),
        in_specs=[vmem] * 8,
        out_specs=(vmem,) * 5,
        scratch_shapes=[
            pltpu.VMEM((SLOTS, half, w), f32),
            pltpu.VMEM((SLOTS, half, w), f32),
            pltpu.VMEM((SLOTS, half, w), f32),
            pltpu.VMEM((SLOTS, half, w), bf),
            pltpu.VMEM((SLOTS, half, w), bf),
            pltpu.VMEM((n_chunks, half, w), f32),
            pltpu.VMEM((n_chunks, half, w), bf),
            pltpu.VMEM((n_chunks, n_out - 1, blk, w), f32),
            pltpu.VMEM((n_chunks, n_out - 1, blk, w), bf),
            pltpu.VMEM((n_chunks, 2, kp_rows, w), bf),
            pltpu.VMEM((SLOTS, 2, half, w), f32),
            pltpu.VMEM((SLOTS, 2, half, w), bf),
            pltpu.VMEM((SLOTS, 2, half, w), bf),
            pltpu.VMEM((n_chunks, 2, half, w), bf),
            pltpu.VMEM((n_chunks, n_out - 1, 2, blk, w), bf),
            pltpu.VMEM((n_chunks, 2, kp_rows, w), bf),
            pltpu.VMEM((2, kp_rows, n_pos), f32),
            pltpu.VMEM((2, kp_rows, n_pos), bf),
            pltpu.VMEM((n_dp - 1, 2, t_rows, n_pos), bf),
            dma((5, SLOTS)),
            dma((5, RECV)),
            dma((5, n_out - 1, SLOTS)),
            dma((5, n_out - 1, RECV)),
            dma((n_dp - 1,)),
            dma((n_dp - 1,)),
        ],
        compiler_params=pltpu.CompilerParams(
            collective_id=0, has_side_effects=True, vmem_limit_bytes=56 * 2**20
        ),
    )(
        query[0], key[0], value[0], grad_ctx[0],
        proj_key, proj_value, proj_key.T, proj_value.T,
    )
    gq, gk, gv, sk, sv = out
    return gq[None], gk[None], gv[None], sk, sv


def solution(mesh):
    return jax.shard_map(
        functools.partial(body, mesh.shape["seq"], mesh.shape["dp"]),
        mesh=mesh,
        in_specs=(
            P("dp", "seq", None),
            P("dp", "seq", None),
            P("dp", "seq", None),
            P("dp", "seq", None),
            P(None, "seq"),
            P(None, "seq"),
        ),
        out_specs=(
            P("dp", "seq", None),
            P("dp", "seq", None),
            P("dp", "seq", None),
            P("dp", "seq"),
            P("dp", "seq"),
        ),
        check_vma=False,
    )
```

```python
import functools

import jax
import jax.numpy as jnp
from jax import lax
from jax.experimental import pallas as pl
from jax.experimental.pallas import tpu as pltpu
from jax.sharding import PartitionSpec as P

HEAD_DIM = 128
INNER = 2
RECV = 8
SLOTS = 8
A, B, C, D, E, F, G, Z, I = 0, 2, 4, 6, 8, 10, 12, 14, 16
NT = (((1,), (1,)), ((), ()))


def dot(a, b):
    return jnp.dot(a, b, preferred_element_type=jnp.float32)


def dot_nt(a, b):
    return lax.dot_general(a, b, NT, preferred_element_type=jnp.float32)


def kernel(
    n_seq, n_dp,
    q_ref, k_ref, v_ref, g_ref, pk_ref, pv_ref,
    gq_ref, gk_ref, gv_ref, sk_ref, sv_ref,
    own_k, own_v, snd_k, snd_v, half_v, arr_k, arr_v, blk_k, blk_v, full,
    own_d, snd_d, half_d, arr_d, blk_d, full_d,
    term, snd_t, arr_t, pkt_ref, pvt_ref,
    s_pair, r_pair, s_grp, r_grp, s_dp, r_dp,
):
    kp_rows = pk_ref.shape[0]
    n_chunks = q_ref.shape[1] // HEAD_DIM
    n_out = n_seq // INNER
    half = kp_rows // INNER
    blk = half // n_out
    t_rows = kp_rows // n_dp
    scale = HEAD_DIM ** (-0.5)
    bf = jnp.bfloat16

    seq = lax.axis_index("seq")
    dp = lax.axis_index("dp")
    x = lax.rem(seq, INNER)
    z = seq // INNER
    mate = seq + 1 - 2 * x
    mine = pl.multiple_of(x * half, half)
    other = pl.multiple_of((1 - x) * half, half)

    def z_at(j):
        return lax.rem(z + j, n_out)

    def peer(j):
        return z_at(j) * INNER + x

    barrier = pltpu.get_barrier_semaphore()
    pl.semaphore_signal(barrier, inc=1, device_id={"seq": mate})
    for j in range(1, n_out):
        pl.semaphore_signal(barrier, inc=1, device_id={"seq": peer(j)})
    for j in range(1, n_dp):
        pl.semaphore_signal(barrier, inc=1, device_id={"dp": lax.rem(dp + j, n_dp)})
    pl.semaphore_wait(barrier, 1 + (n_out - 1) + (n_dp - 1))

    def cols(c):
        return pl.ds(pl.multiple_of(c * HEAD_DIM, HEAD_DIM), HEAD_DIM)

    def pair_copy(kind, src, dst, c):
        return pltpu.make_async_remote_copy(
            src_ref=src, dst_ref=dst,
            send_sem=s_pair.at[kind, lax.rem(c, SLOTS)],
            recv_sem=r_pair.at[kind, lax.rem(c, RECV)],
            device_id={"seq": mate},
        )

    def grp_copy(kind, j, src, dst, c):
        return pltpu.make_async_remote_copy(
            src_ref=src, dst_ref=dst,
            send_sem=s_grp.at[kind, j - 1, lax.rem(c, SLOTS)],
            recv_sem=r_grp.at[kind, j - 1, lax.rem(c, RECV)],
            device_id={"seq": peer(j)},
        )

    def a_copies(c):
        s = lax.rem(c, SLOTS)
        return [
            pair_copy(0, snd_k.at[s], arr_k.at[c], c),
            pair_copy(1, snd_v.at[s], arr_v.at[c], c),
        ]

    def b_copies(c):
        s = lax.rem(c, SLOTS)
        out = []
        for j in range(1, n_out):
            rows = pl.ds(pl.multiple_of(z_at(j) * blk, blk), blk)
            out.append(grp_copy(0, j, own_k.at[s, rows], blk_k.at[c, j - 1], c))
            out.append(grp_copy(1, j, half_v.at[s, rows], blk_v.at[c, j - 1], c))
        return out

    own_rows = pl.ds(pl.multiple_of(x * half + z * blk, blk), blk)
    half_rows = pl.ds(mine, half)
    in_half = pl.ds(pl.multiple_of(z * blk, blk), blk)

    def gather_copies(kind, buf, c):
        ref = buf.at[c, :, own_rows]
        return [grp_copy(kind, j, ref, ref, c) for j in range(1, n_out)]

    def mate_copies(kind, buf, c):
        ref = buf.at[c, :, half_rows]
        return [pair_copy(kind, ref, ref, c)]

    def e_copies(c):
        return [pair_copy(3, snd_d.at[lax.rem(c, SLOTS)], arr_d.at[c], c)]

    def f_copies(c):
        s = lax.rem(c, SLOTS)
        out = []
        for j in range(1, n_out):
            rows = pl.ds(pl.multiple_of(z_at(j) * blk, blk), blk)
            out.append(grp_copy(3, j, half_d.at[s, :, rows], blk_d.at[c, j - 1], c))
        return out

    def start(copies):
        for copy in copies:
            copy.start()

    def wait(copies):
        for copy in copies:
            copy.wait()

    def stage_a(c):
        s = lax.rem(c, SLOTS)
        kc = k_ref[:, cols(c)]
        vc = v_ref[:, cols(c)]
        snd_k[s] = dot(pk_ref[pl.ds(other, half), :], kc)
        snd_v[s] = dot(pv_ref[pl.ds(other, half), :], vc).astype(bf)
        start(a_copies(c))
        own_k[s] = dot(pk_ref[pl.ds(mine, half), :], kc)
        own_v[s] = dot(pv_ref[pl.ds(mine, half), :], vc)

    def stage_b(c):
        s = lax.rem(c, SLOTS)
        wait(a_copies(c))
        own_k[s] = own_k[s] + arr_k[c]
        both = own_v[s] + arr_v[c].astype(jnp.float32)
        own_v[s] = both
        half_v[s] = both.astype(bf)
        start(b_copies(c))

    def stage_c(c):
        s = lax.rem(c, SLOTS)
        wait(b_copies(c))
        kt = own_k[s, in_half]
        vt = own_v[s, in_half]
        for j in range(1, n_out):
            kt += blk_k[c, j - 1]
            vt += blk_v[c, j - 1].astype(jnp.float32)
        full[c, 0, own_rows] = kt.astype(bf)
        full[c, 1, own_rows] = vt.astype(bf)
        start(gather_copies(2, full, c))

    def stage_d(c):
        wait(gather_copies(2, full, c))
        start(mate_copies(2, full, c))

    def stage_e(c):
        s = lax.rem(c, SLOTS)
        wait(mate_copies(2, full, c))
        kp = full[c, 0]
        vp = full[c, 1]
        kpt = kp.astype(jnp.float32).T.astype(bf)
        n_pos = q_ref.shape[0]
        step = min(256, n_pos)
        dk = jnp.zeros((kp_rows, HEAD_DIM), jnp.float32)
        dv = jnp.zeros((kp_rows, HEAD_DIM), jnp.float32)
        for p in range(0, n_pos, step):
            qb = q_ref[pl.ds(p, step), cols(c)]
            gb = g_ref[pl.ds(p, step), cols(c)]
            scores = dot_nt(kp, qb) * scale
            e = jnp.exp(scores - jnp.max(scores, axis=0, keepdims=True))
            probs = e * (1.0 / jnp.sum(e, axis=0, keepdims=True))
            dv += dot(probs.astype(bf), gb)
            gp = dot_nt(vp, gb)
            delta = jnp.sum(probs * gp, axis=0, keepdims=True)
            gs = (probs * (gp - delta) * scale).astype(bf)
            dk += dot(gs, qb)
            gq_ref[pl.ds(p, step), cols(c)] = dot(kpt, gs).T.astype(bf)
        own_d[s, 0] = jnp.where(x == 0, dk[:half], dk[half:])
        own_d[s, 1] = jnp.where(x == 0, dv[:half], dv[half:])
        snd_d[s, 0] = jnp.where(x == 0, dk[half:], dk[:half]).astype(bf)
        snd_d[s, 1] = jnp.where(x == 0, dv[half:], dv[:half]).astype(bf)
        start(e_copies(c))

    def stage_f(c):
        s = lax.rem(c, SLOTS)
        wait(e_copies(c))
        both = own_d[s] + arr_d[c].astype(jnp.float32)
        own_d[s] = both
        half_d[s] = both.astype(bf)
        start(f_copies(c))

    def stage_g(c):
        s = lax.rem(c, SLOTS)
        wait(f_copies(c))
        total = own_d[s, :, in_half]
        for j in range(1, n_out):
            total += blk_d[c, j - 1].astype(jnp.float32)
        full_d[c, :, own_rows] = total.astype(bf)
        start(gather_copies(4, full_d, c))

    def stage_z(c):
        wait(gather_copies(4, full_d, c))
        start(mate_copies(4, full_d, c))

    def stage_i(c):
        wait(mate_copies(4, full_d, c))
        dkp = full_d[c, 0]
        dvp = full_d[c, 1]
        gk_ref[:, cols(c)] = dot(pkt_ref[...], dkp).astype(bf)
        gv_ref[:, cols(c)] = dot(pvt_ref[...], dvp).astype(bf)
        term[0] += dot_nt(dkp, k_ref[:, cols(c)])
        term[1] += dot_nt(dvp, v_ref[:, cols(c)])

    term[...] = jnp.zeros_like(term)

    stages = (
        (A, stage_a), (Z, stage_z), (D, stage_d), (G, stage_g), (F, stage_f), (C, stage_c),
        (B, stage_b), (E, stage_e), (I, stage_i),
    )

    def turn():
        pkt_ref[...] = pk_ref[...].astype(jnp.float32).T.astype(bf)
        pvt_ref[...] = pv_ref[...].astype(jnp.float32).T.astype(bf)

    def iteration(i, _):
        pl.when(i == 1)(turn)
        for at, stage in stages:
            pl.when((i >= at) & (i < at + n_chunks))(functools.partial(stage, i - at))
        return 0

    lax.fori_loop(0, n_chunks + I, iteration, 0)

    snd_t[...] = term[...].astype(bf)
    copies = []
    for j in range(1, n_dp):
        to = lax.rem(dp + j, n_dp)
        rows = pl.ds(pl.multiple_of(to * t_rows, t_rows), t_rows)
        copies.append(
            pltpu.make_async_remote_copy(
                src_ref=snd_t.at[:, rows], dst_ref=arr_t.at[j - 1],
                send_sem=s_dp.at[j - 1], recv_sem=r_dp.at[j - 1],
                device_id={"dp": to},
            )
        )
    start(copies)
    wait(copies)
    total = term[:, pl.ds(pl.multiple_of(dp * t_rows, t_rows), t_rows)]
    for j in range(1, n_dp):
        total += arr_t[j - 1].astype(jnp.float32)
    sk_ref[...] = total[0].astype(bf)
    sv_ref[...] = total[1].astype(bf)


def body(n_seq, n_dp, query, key, value, grad_ctx, proj_key, proj_value):
    _, n_pos, hd = query.shape
    kp_rows = proj_key.shape[0]
    n_chunks = hd // HEAD_DIM
    n_out = n_seq // INNER
    half = kp_rows // INNER
    blk = half // n_out
    t_rows = kp_rows // n_dp
    w = HEAD_DIM
    f32, bf = jnp.float32, jnp.bfloat16
    dma = pltpu.SemaphoreType.DMA
    vmem = pl.BlockSpec(memory_space=pltpu.VMEM)
    wide = jax.ShapeDtypeStruct((n_pos, hd), bf)
    tall = jax.ShapeDtypeStruct((t_rows, n_pos), bf)
    out = pl.pallas_call(
        functools.partial(kernel, n_seq, n_dp),
        out_shape=(wide, wide, wide, tall, tall),
        in_specs=[vmem] * 6,
        out_specs=(vmem,) * 5,
        scratch_shapes=[
            pltpu.VMEM((SLOTS, half, w), f32),
            pltpu.VMEM((SLOTS, half, w), f32),
            pltpu.VMEM((SLOTS, half, w), f32),
            pltpu.VMEM((SLOTS, half, w), bf),
            pltpu.VMEM((SLOTS, half, w), bf),
            pltpu.VMEM((n_chunks, half, w), f32),
            pltpu.VMEM((n_chunks, half, w), bf),
            pltpu.VMEM((n_chunks, n_out - 1, blk, w), f32),
            pltpu.VMEM((n_chunks, n_out - 1, blk, w), bf),
            pltpu.VMEM((n_chunks, 2, kp_rows, w), bf),
            pltpu.VMEM((SLOTS, 2, half, w), f32),
            pltpu.VMEM((SLOTS, 2, half, w), bf),
            pltpu.VMEM((SLOTS, 2, half, w), bf),
            pltpu.VMEM((n_chunks, 2, half, w), bf),
            pltpu.VMEM((n_chunks, n_out - 1, 2, blk, w), bf),
            pltpu.VMEM((n_chunks, 2, kp_rows, w), bf),
            pltpu.VMEM((2, kp_rows, n_pos), f32),
            pltpu.VMEM((2, kp_rows, n_pos), bf),
            pltpu.VMEM((n_dp - 1, 2, t_rows, n_pos), bf),
            pltpu.VMEM((n_pos, kp_rows), bf),
            pltpu.VMEM((n_pos, kp_rows), bf),
            dma((5, SLOTS)),
            dma((5, RECV)),
            dma((5, n_out - 1, SLOTS)),
            dma((5, n_out - 1, RECV)),
            dma((n_dp - 1,)),
            dma((n_dp - 1,)),
        ],
        compiler_params=pltpu.CompilerParams(
            collective_id=0, has_side_effects=True, vmem_limit_bytes=56 * 2**20
        ),
    )(
        query[0], key[0], value[0], grad_ctx[0],
        proj_key, proj_value,
    )
    gq, gk, gv, sk, sv = out
    return gq[None], gk[None], gv[None], sk, sv


def solution(mesh):
    return jax.shard_map(
        functools.partial(body, mesh.shape["seq"], mesh.shape["dp"]),
        mesh=mesh,
        in_specs=(
            P("dp", "seq", None),
            P("dp", "seq", None),
            P("dp", "seq", None),
            P("dp", "seq", None),
            P(None, "seq"),
            P(None, "seq"),
        ),
        out_specs=(
            P("dp", "seq", None),
            P("dp", "seq", None),
            P("dp", "seq", None),
            P("dp", "seq"),
            P("dp", "seq"),
        ),
        check_vma=False,
    )
```

```python
import functools

import jax
import jax.numpy as jnp
from jax import lax
from jax.experimental import pallas as pl
from jax.experimental.pallas import tpu as pltpu
from jax.sharding import PartitionSpec as P

HEAD_DIM = 128
ROOM = 2
NT = (((1,), (1,)), ((), ()))


def dot(a, b):
    return jnp.dot(a, b, preferred_element_type=jnp.float32)


def dot_nt(a, b):
    return lax.dot_general(a, b, NT, preferred_element_type=jnp.float32)


def n_bits(n_seq):
    return n_seq.bit_length() - 1


def n_slots(n_seq):
    return ROOM * n_bits(n_seq) + 2


def kernel(
    n_seq, n_dp,
    q_ref, k_ref, v_ref, g_ref, pk_ref, pv_ref,
    gq_ref, gk_ref, gv_ref, sk_ref, sv_ref,
    acc_k, acc_v, snd_v, arr_k, arr_v, full,
    acc_d, snd_d, arr_d, full_d,
    term, snd_t, arr_t, pkt_ref, pvt_ref,
    s_sem, r_sem, s_dp, r_dp,
):
    kp_rows = pk_ref.shape[0]
    n_chunks = q_ref.shape[1] // HEAD_DIM
    nb = n_bits(n_seq)
    slots = n_slots(n_seq)
    t_rows = kp_rows // n_dp
    scale = HEAD_DIM ** (-0.5)
    bf = jnp.bfloat16

    seq = lax.axis_index("seq")
    dp = lax.axis_index("dp")
    bits = [lax.rem(seq // (1 << b), 2) for b in range(nb)]
    mates = [seq + (1 - 2 * bits[b]) * (1 << b) for b in range(nb)]

    barrier = pltpu.get_barrier_semaphore()
    for b in range(nb):
        pl.semaphore_signal(barrier, inc=1, device_id={"seq": mates[b]})
    for j in range(1, n_dp):
        pl.semaphore_signal(barrier, inc=1, device_id={"dp": lax.rem(dp + j, n_dp)})
    pl.semaphore_wait(barrier, nb + n_dp - 1)

    def cols(c):
        return pl.ds(pl.multiple_of(c * HEAD_DIM, HEAD_DIM), HEAD_DIM)

    def route(c):
        t = lax.rem(c, 4) // 3
        pick = lambda a, l: [a[0] + t * (a[1] - a[0]), a[1] + t * (a[0] - a[1])] + l
        return pick(bits, bits[2:]), pick(mates, mates[2:])

    def size(s):
        return kp_rows >> (s + 1)

    def rows_at(off, s):
        return pl.ds(pl.multiple_of(off, size(s)), size(s))

    def keep(c, s):
        bit, _ = route(c)
        return rows_at(sum(bit[i] * size(i) for i in range(s + 1)), s)

    def give(c, s):
        bit, _ = route(c)
        return rows_at(sum(bit[i] * size(i) for i in range(s)) + (1 - bit[s]) * size(s), s)

    def landing(s):
        return pl.ds(kp_rows - (kp_rows >> s), size(s))

    def copy(kind, s, c, src, dst):
        slot = lax.rem(c, slots)
        return pltpu.make_async_remote_copy(
            src_ref=src, dst_ref=dst,
            send_sem=s_sem.at[kind, s, slot],
            recv_sem=r_sem.at[kind, s, slot],
            device_id={"seq": route(c)[1][s]},
        )

    def kv_copies(c, s):
        slot = lax.rem(c, slots)
        return [
            copy(0, s, c, acc_k.at[slot, give(c, s)], arr_k.at[c, landing(s)]),
            copy(1, s, c, snd_v.at[slot, give(c, s)], arr_v.at[c, landing(s)]),
        ]

    def d_copies(c, s):
        slot = lax.rem(c, slots)
        return [copy(3, s, c, snd_d.at[slot, :, give(c, s)], arr_d.at[c, :, landing(s)])]

    def gather_copies(kind, buf, c, s):
        ref = buf.at[c, :, keep(c, s)]
        return [copy(kind, s, c, ref, ref)]

    def start(copies):
        for one in copies:
            one.start()

    def wait(copies):
        for one in copies:
            one.wait()

    def send_kv(c, s):
        slot = lax.rem(c, slots)
        snd_v[slot, give(c, s)] = acc_v[slot, give(c, s)].astype(bf)
        start(kv_copies(c, s))

    def send_d(c, s):
        slot = lax.rem(c, slots)
        snd_d[slot, :, give(c, s)] = acc_d[slot, :, give(c, s)].astype(bf)
        start(d_copies(c, s))

    def stage_a(c):
        slot = lax.rem(c, slots)
        acc_k[slot] = dot(pk_ref[...], k_ref[:, cols(c)])
        acc_v[slot] = dot(pv_ref[...], v_ref[:, cols(c)])
        send_kv(c, 0)

    def sum_kv(s, c):
        slot = lax.rem(c, slots)
        wait(kv_copies(c, s))
        rows = keep(c, s)
        kt = acc_k[slot, rows] + arr_k[c, landing(s)]
        vt = acc_v[slot, rows] + arr_v[c, landing(s)].astype(jnp.float32)
        if s < nb - 1:
            acc_k[slot, rows] = kt
            acc_v[slot, rows] = vt
            send_kv(c, s + 1)
        else:
            full[c, 0, rows] = kt.astype(bf)
            full[c, 1, rows] = vt.astype(bf)
            start(gather_copies(2, full, c, s))

    def sum_d(s, c):
        slot = lax.rem(c, slots)
        wait(d_copies(c, s))
        rows = keep(c, s)
        total = acc_d[slot, :, rows] + arr_d[c, :, landing(s)].astype(jnp.float32)
        if s < nb - 1:
            acc_d[slot, :, rows] = total
            send_d(c, s + 1)
        else:
            full_d[c, :, rows] = total.astype(bf)
            start(gather_copies(4, full_d, c, s))

    def gather(kind, buf, s, c):
        wait(gather_copies(kind, buf, c, s))
        start(gather_copies(kind, buf, c, s - 1))

    def stage_e(c):
        slot = lax.rem(c, slots)
        wait(gather_copies(2, full, c, 0))
        kp = full[c, 0]
        vp = full[c, 1]
        kpt = kp.astype(jnp.float32).T.astype(bf)
        n_pos = q_ref.shape[0]
        step = min(256, n_pos)
        dk = jnp.zeros((kp_rows, HEAD_DIM), jnp.float32)
        dv = jnp.zeros((kp_rows, HEAD_DIM), jnp.float32)
        for p in range(0, n_pos, step):
            qb = q_ref[pl.ds(p, step), cols(c)]
            gb = g_ref[pl.ds(p, step), cols(c)]
            scores = dot_nt(kp, qb) * scale
            e = jnp.exp(scores - jnp.max(scores, axis=0, keepdims=True))
            probs = e * (1.0 / jnp.sum(e, axis=0, keepdims=True))
            dv += dot(probs.astype(bf), gb)
            gp = dot_nt(vp, gb)
            delta = jnp.sum(probs * gp, axis=0, keepdims=True)
            gs = (probs * (gp - delta) * scale).astype(bf)
            dk += dot(gs, qb)
            gq_ref[pl.ds(p, step), cols(c)] = dot(kpt, gs).T.astype(bf)
        acc_d[slot, 0] = dk
        acc_d[slot, 1] = dv
        send_d(c, 0)

    def stage_i(c):
        wait(gather_copies(4, full_d, c, 0))
        dkp = full_d[c, 0]
        dvp = full_d[c, 1]
        gk_ref[:, cols(c)] = dot(pkt_ref[...], dkp).astype(bf)
        gv_ref[:, cols(c)] = dot(pvt_ref[...], dvp).astype(bf)
        term[0] += dot_nt(dkp, k_ref[:, cols(c)])
        term[1] += dot_nt(dvp, v_ref[:, cols(c)])

    term[...] = jnp.zeros_like(term)

    def turn():
        pkt_ref[...] = pk_ref[...].astype(jnp.float32).T.astype(bf)
        pvt_ref[...] = pv_ref[...].astype(jnp.float32).T.astype(bf)

    stages = [stage_a]
    stages += [functools.partial(sum_kv, s) for s in range(nb)]
    stages += [functools.partial(gather, 2, full, s) for s in range(nb - 1, 0, -1)]
    stages += [stage_e]
    stages += [functools.partial(sum_d, s) for s in range(nb)]
    stages += [functools.partial(gather, 4, full_d, s) for s in range(nb - 1, 0, -1)]
    stages += [stage_i]
    heavy = (stage_e, stage_i)
    placed = list(enumerate(stages))
    order = [p for p in reversed(placed) if p[1] not in heavy] + [p for p in placed if p[1] in heavy]

    def iteration(i, _):
        pl.when(i == 1)(turn)
        for n, stage in order:
            at = n * ROOM
            pl.when((i >= at) & (i < at + n_chunks))(functools.partial(stage, i - at))
        return 0

    lax.fori_loop(0, n_chunks + ROOM * (len(stages) - 1), iteration, 0)

    snd_t[...] = term[...].astype(bf)
    copies = []
    for j in range(1, n_dp):
        to = lax.rem(dp + j, n_dp)
        rows = pl.ds(pl.multiple_of(to * t_rows, t_rows), t_rows)
        copies.append(
            pltpu.make_async_remote_copy(
                src_ref=snd_t.at[:, rows], dst_ref=arr_t.at[j - 1],
                send_sem=s_dp.at[j - 1], recv_sem=r_dp.at[j - 1],
                device_id={"dp": to},
            )
        )
    start(copies)
    wait(copies)
    total = term[:, pl.ds(pl.multiple_of(dp * t_rows, t_rows), t_rows)]
    for j in range(1, n_dp):
        total += arr_t[j - 1].astype(jnp.float32)
    sk_ref[...] = total[0].astype(bf)
    sv_ref[...] = total[1].astype(bf)


def body(n_seq, n_dp, query, key, value, grad_ctx, proj_key, proj_value):
    _, n_pos, hd = query.shape
    kp_rows = proj_key.shape[0]
    n_chunks = hd // HEAD_DIM
    nb = n_bits(n_seq)
    slots = n_slots(n_seq)
    t_rows = kp_rows // n_dp
    w = HEAD_DIM
    f32, bf = jnp.float32, jnp.bfloat16
    dma = pltpu.SemaphoreType.DMA
    vmem = pl.BlockSpec(memory_space=pltpu.VMEM)
    wide = jax.ShapeDtypeStruct((n_pos, hd), bf)
    tall = jax.ShapeDtypeStruct((t_rows, n_pos), bf)
    out = pl.pallas_call(
        functools.partial(kernel, n_seq, n_dp),
        out_shape=(wide, wide, wide, tall, tall),
        in_specs=[vmem] * 6,
        out_specs=(vmem,) * 5,
        scratch_shapes=[
            pltpu.VMEM((slots, kp_rows, w), f32),
            pltpu.VMEM((slots, kp_rows, w), f32),
            pltpu.VMEM((slots, kp_rows, w), bf),
            pltpu.VMEM((n_chunks, kp_rows, w), f32),
            pltpu.VMEM((n_chunks, kp_rows, w), bf),
            pltpu.VMEM((n_chunks, 2, kp_rows, w), bf),
            pltpu.VMEM((slots, 2, kp_rows, w), f32),
            pltpu.VMEM((slots, 2, kp_rows, w), bf),
            pltpu.VMEM((n_chunks, 2, kp_rows, w), bf),
            pltpu.VMEM((n_chunks, 2, kp_rows, w), bf),
            pltpu.VMEM((2, kp_rows, n_pos), f32),
            pltpu.VMEM((2, kp_rows, n_pos), bf),
            pltpu.VMEM((n_dp - 1, 2, t_rows, n_pos), bf),
            pltpu.VMEM((n_pos, kp_rows), bf),
            pltpu.VMEM((n_pos, kp_rows), bf),
            dma((5, nb, slots)),
            dma((5, nb, slots)),
            dma((n_dp - 1,)),
            dma((n_dp - 1,)),
        ],
        compiler_params=pltpu.CompilerParams(
            collective_id=0, has_side_effects=True, vmem_limit_bytes=60 * 2**20
        ),
    )(
        query[0], key[0], value[0], grad_ctx[0],
        proj_key, proj_value,
    )
    gq, gk, gv, sk, sv = out
    return gq[None], gk[None], gv[None], sk, sv


def solution(mesh):
    return jax.shard_map(
        functools.partial(body, mesh.shape["seq"], mesh.shape["dp"]),
        mesh=mesh,
        in_specs=(
            P("dp", "seq", None),
            P("dp", "seq", None),
            P("dp", "seq", None),
            P("dp", "seq", None),
            P(None, "seq"),
            P(None, "seq"),
        ),
        out_specs=(
            P("dp", "seq", None),
            P("dp", "seq", None),
            P("dp", "seq", None),
            P("dp", "seq"),
            P("dp", "seq"),
        ),
        check_vma=False,
    )
```

```python
import functools

import jax
import jax.numpy as jnp
from jax import lax
from jax.experimental import pallas as pl
from jax.experimental.pallas import tpu as pltpu
from jax.sharding import PartitionSpec as P

HEAD_DIM = 128
ROOM = 1
NT = (((1,), (1,)), ((), ()))


def dot(a, b):
    return jnp.dot(a, b, preferred_element_type=jnp.float32)


def dot_nt(a, b):
    return lax.dot_general(a, b, NT, preferred_element_type=jnp.float32)


def n_bits(n_seq):
    return n_seq.bit_length() - 1


def n_slots(n_seq):
    return ROOM * n_bits(n_seq) + 5


def kernel(
    n_seq, n_dp,
    q_ref, k_ref, v_ref, g_ref, pk_ref, pv_ref,
    gq_ref, gk_ref, gv_ref, sk_ref, sv_ref,
    acc_k, acc_v, snd_v, arr_k, arr_v, full,
    acc_d, snd_d, arr_d, full_d,
    term, snd_t, arr_t, pkt_ref, pvt_ref,
    s_sem, r_sem, s_dp, r_dp,
):
    kp_rows = pk_ref.shape[0]
    n_chunks = q_ref.shape[1] // HEAD_DIM
    nb = n_bits(n_seq)
    slots = n_slots(n_seq)
    t_rows = kp_rows // n_dp
    scale = HEAD_DIM ** (-0.5)
    bf = jnp.bfloat16

    seq = lax.axis_index("seq")
    dp = lax.axis_index("dp")
    bits = [lax.rem(seq // (1 << b), 2) for b in range(nb)]
    mates = [seq + (1 - 2 * bits[b]) * (1 << b) for b in range(nb)]

    barrier = pltpu.get_barrier_semaphore()
    for b in range(nb):
        pl.semaphore_signal(barrier, inc=1, device_id={"seq": mates[b]})
    for j in range(1, n_dp):
        pl.semaphore_signal(barrier, inc=1, device_id={"dp": lax.rem(dp + j, n_dp)})
    pl.semaphore_wait(barrier, nb + n_dp - 1)

    def cols(c):
        return pl.ds(pl.multiple_of(c * HEAD_DIM, HEAD_DIM), HEAD_DIM)

    def route(c):
        t = lax.rem(c, 4) // 3
        pick = lambda a, l: [a[0] + t * (a[1] - a[0]), a[1] + t * (a[0] - a[1])] + l
        return pick(bits, bits[2:]), pick(mates, mates[2:])

    def size(s):
        return kp_rows >> (s + 1)

    def rows_at(off, s):
        return pl.ds(pl.multiple_of(off, size(s)), size(s))

    def keep(c, s):
        bit, _ = route(c)
        return rows_at(sum(bit[i] * size(i) for i in range(s + 1)), s)

    def give(c, s):
        bit, _ = route(c)
        return rows_at(sum(bit[i] * size(i) for i in range(s)) + (1 - bit[s]) * size(s), s)

    def landing(s):
        return pl.ds(kp_rows - (kp_rows >> s), size(s))

    def copy(kind, s, c, src, dst):
        slot = lax.rem(c, slots)
        return pltpu.make_async_remote_copy(
            src_ref=src, dst_ref=dst,
            send_sem=s_sem.at[kind, s, slot],
            recv_sem=r_sem.at[kind, s, slot],
            device_id={"seq": route(c)[1][s]},
        )

    def kv_copies(c, s):
        slot = lax.rem(c, slots)
        return [
            copy(0, s, c, acc_k.at[slot, give(c, s)], arr_k.at[c, landing(s)]),
            copy(1, s, c, snd_v.at[slot, give(c, s)], arr_v.at[c, landing(s)]),
        ]

    def d_copies(c, s):
        slot = lax.rem(c, slots)
        return [copy(3, s, c, snd_d.at[slot, :, give(c, s)], arr_d.at[c, :, landing(s)])]

    def gather_copies(kind, buf, c, s):
        ref = buf.at[c, :, keep(c, s)]
        return [copy(kind, s, c, ref, ref)]

    def start(copies):
        for one in copies:
            one.start()

    def wait(copies):
        for one in copies:
            one.wait()

    def send_kv(c, s):
        slot = lax.rem(c, slots)
        snd_v[slot, give(c, s)] = acc_v[slot, give(c, s)].astype(bf)
        start(kv_copies(c, s))

    def send_d(c, s):
        slot = lax.rem(c, slots)
        snd_d[slot, :, give(c, s)] = acc_d[slot, :, give(c, s)].astype(bf)
        start(d_copies(c, s))

    def stage_a(c):
        slot = lax.rem(c, slots)
        acc_k[slot] = dot(pk_ref[...], k_ref[:, cols(c)])
        acc_v[slot] = dot(pv_ref[...], v_ref[:, cols(c)])
        send_kv(c, 0)

    def sum_kv(s, c):
        slot = lax.rem(c, slots)
        wait(kv_copies(c, s))
        rows = keep(c, s)
        kt = acc_k[slot, rows] + arr_k[c, landing(s)]
        vt = acc_v[slot, rows] + arr_v[c, landing(s)].astype(jnp.float32)
        if s < nb - 1:
            acc_k[slot, rows] = kt
            acc_v[slot, rows] = vt
            send_kv(c, s + 1)
        else:
            full[c, 0, rows] = kt.astype(bf)
            full[c, 1, rows] = vt.astype(bf)
            start(gather_copies(2, full, c, s))

    def sum_d(s, c):
        slot = lax.rem(c, slots)
        wait(d_copies(c, s))
        rows = keep(c, s)
        total = acc_d[slot, :, rows] + arr_d[c, :, landing(s)].astype(jnp.float32)
        if s < nb - 1:
            acc_d[slot, :, rows] = total
            send_d(c, s + 1)
        else:
            full_d[c, :, rows] = total.astype(bf)
            start(gather_copies(4, full_d, c, s))

    def gather(kind, buf, s, c):
        wait(gather_copies(kind, buf, c, s))
        start(gather_copies(kind, buf, c, s - 1))

    def stage_e(c):
        slot = lax.rem(c, slots)
        wait(gather_copies(2, full, c, 0))
        kp = full[c, 0]
        vp = full[c, 1]
        kpt = kp.astype(jnp.float32).T.astype(bf)
        n_pos = q_ref.shape[0]
        step = min(256, n_pos)
        dk = jnp.zeros((kp_rows, HEAD_DIM), jnp.float32)
        dv = jnp.zeros((kp_rows, HEAD_DIM), jnp.float32)
        for p in range(0, n_pos, step):
            qb = q_ref[pl.ds(p, step), cols(c)]
            gb = g_ref[pl.ds(p, step), cols(c)]
            scores = dot_nt(kp, qb) * scale
            e = jnp.exp(scores - jnp.max(scores, axis=0, keepdims=True))
            probs = e * (1.0 / jnp.sum(e, axis=0, keepdims=True))
            dv += dot(probs.astype(bf), gb)
            gp = dot_nt(vp, gb)
            delta = jnp.sum(probs * gp, axis=0, keepdims=True)
            gs = (probs * (gp - delta) * scale).astype(bf)
            dk += dot(gs, qb)
            gq_ref[pl.ds(p, step), cols(c)] = dot(kpt, gs).T.astype(bf)
        acc_d[slot, 0] = dk
        acc_d[slot, 1] = dv
        send_d(c, 0)

    def stage_i(c):
        wait(gather_copies(4, full_d, c, 0))
        dkp = full_d[c, 0]
        dvp = full_d[c, 1]
        gk_ref[:, cols(c)] = dot(pkt_ref[...], dkp).astype(bf)
        gv_ref[:, cols(c)] = dot(pvt_ref[...], dvp).astype(bf)
        term[0] += dot_nt(dkp, k_ref[:, cols(c)])
        term[1] += dot_nt(dvp, v_ref[:, cols(c)])

    term[...] = jnp.zeros_like(term)

    def turn():
        pkt_ref[...] = pk_ref[...].astype(jnp.float32).T.astype(bf)
        pvt_ref[...] = pv_ref[...].astype(jnp.float32).T.astype(bf)

    stages = [stage_a]
    stages += [functools.partial(sum_kv, s) for s in range(nb)]
    stages += [functools.partial(gather, 2, full, s) for s in range(nb - 1, 0, -1)]
    stages += [stage_e]
    stages += [functools.partial(sum_d, s) for s in range(nb)]
    stages += [functools.partial(gather, 4, full_d, s) for s in range(nb - 1, 0, -1)]
    stages += [stage_i]
    def iteration(i, _):
        pl.when(i == 1)(turn)
        for n, stage in enumerate(stages):
            at = n * ROOM
            pl.when((i >= at) & (i < at + n_chunks))(functools.partial(stage, i - at))
        return 0

    lax.fori_loop(0, n_chunks + ROOM * (len(stages) - 1), iteration, 0)

    snd_t[...] = term[...].astype(bf)
    copies = []
    for j in range(1, n_dp):
        to = lax.rem(dp + j, n_dp)
        rows = pl.ds(pl.multiple_of(to * t_rows, t_rows), t_rows)
        copies.append(
            pltpu.make_async_remote_copy(
                src_ref=snd_t.at[:, rows], dst_ref=arr_t.at[j - 1],
                send_sem=s_dp.at[j - 1], recv_sem=r_dp.at[j - 1],
                device_id={"dp": to},
            )
        )
    start(copies)
    wait(copies)
    total = term[:, pl.ds(pl.multiple_of(dp * t_rows, t_rows), t_rows)]
    for j in range(1, n_dp):
        total += arr_t[j - 1].astype(jnp.float32)
    sk_ref[...] = total[0].astype(bf)
    sv_ref[...] = total[1].astype(bf)


def body(n_seq, n_dp, query, key, value, grad_ctx, proj_key, proj_value):
    _, n_pos, hd = query.shape
    kp_rows = proj_key.shape[0]
    n_chunks = hd // HEAD_DIM
    nb = n_bits(n_seq)
    slots = n_slots(n_seq)
    t_rows = kp_rows // n_dp
    w = HEAD_DIM
    f32, bf = jnp.float32, jnp.bfloat16
    dma = pltpu.SemaphoreType.DMA
    vmem = pl.BlockSpec(memory_space=pltpu.VMEM)
    wide = jax.ShapeDtypeStruct((n_pos, hd), bf)
    tall = jax.ShapeDtypeStruct((t_rows, n_pos), bf)
    out = pl.pallas_call(
        functools.partial(kernel, n_seq, n_dp),
        out_shape=(wide, wide, wide, tall, tall),
        in_specs=[vmem] * 6,
        out_specs=(vmem,) * 5,
        scratch_shapes=[
            pltpu.VMEM((slots, kp_rows, w), f32),
            pltpu.VMEM((slots, kp_rows, w), f32),
            pltpu.VMEM((slots, kp_rows, w), bf),
            pltpu.VMEM((n_chunks, kp_rows, w), f32),
            pltpu.VMEM((n_chunks, kp_rows, w), bf),
            pltpu.VMEM((n_chunks, 2, kp_rows, w), bf),
            pltpu.VMEM((slots, 2, kp_rows, w), f32),
            pltpu.VMEM((slots, 2, kp_rows, w), bf),
            pltpu.VMEM((n_chunks, 2, kp_rows, w), bf),
            pltpu.VMEM((n_chunks, 2, kp_rows, w), bf),
            pltpu.VMEM((2, kp_rows, n_pos), f32),
            pltpu.VMEM((2, kp_rows, n_pos), bf),
            pltpu.VMEM((n_dp - 1, 2, t_rows, n_pos), bf),
            pltpu.VMEM((n_pos, kp_rows), bf),
            pltpu.VMEM((n_pos, kp_rows), bf),
            dma((5, nb, slots)),
            dma((5, nb, slots)),
            dma((n_dp - 1,)),
            dma((n_dp - 1,)),
        ],
        compiler_params=pltpu.CompilerParams(
            collective_id=0, has_side_effects=True, vmem_limit_bytes=60 * 2**20
        ),
    )(
        query[0], key[0], value[0], grad_ctx[0],
        proj_key, proj_value,
    )
    gq, gk, gv, sk, sv = out
    return gq[None], gk[None], gv[None], sk, sv


def solution(mesh):
    return jax.shard_map(
        functools.partial(body, mesh.shape["seq"], mesh.shape["dp"]),
        mesh=mesh,
        in_specs=(
            P("dp", "seq", None),
            P("dp", "seq", None),
            P("dp", "seq", None),
            P("dp", "seq", None),
            P(None, "seq"),
            P(None, "seq"),
        ),
        out_specs=(
            P("dp", "seq", None),
            P("dp", "seq", None),
            P("dp", "seq", None),
            P("dp", "seq"),
            P("dp", "seq"),
        ),
        check_vma=False,
    )
```

```python
import functools

import jax
import jax.numpy as jnp
from jax import lax
from jax.experimental import pallas as pl
from jax.experimental.pallas import tpu as pltpu
from jax.sharding import PartitionSpec as P

HEAD_DIM = 128
NT = (((1,), (1,)), ((), ()))


def dot(a, b):
    return jnp.dot(a, b, preferred_element_type=jnp.float32)


def dot_nt(a, b):
    return lax.dot_general(a, b, NT, preferred_element_type=jnp.float32)


def n_bits(n_seq):
    return n_seq.bit_length() - 1


def n_slots(n_seq):
    return n_bits(n_seq) + 5


def kernel(
    n_seq, n_dp,
    q_ref, k_ref, v_ref, g_ref, pk_ref, pv_ref,
    gq_ref, gk_ref, gv_ref, sk_ref, sv_ref,
    acc_k, acc_v, snd_v, arr_k, arr_v, full,
    acc_d, snd_d, arr_d, full_d,
    term, snd_t, arr_t, pkt_ref, pvt_ref,
    s_sem, r_sem, s_dp, r_dp,
):
    kp_rows = pk_ref.shape[0]
    n_chunks = q_ref.shape[1] // HEAD_DIM
    nb = n_bits(n_seq)
    slots = n_slots(n_seq)
    t_rows = kp_rows // n_dp
    scale = HEAD_DIM ** (-0.5)
    bf = jnp.bfloat16

    seq = lax.axis_index("seq")
    dp = lax.axis_index("dp")
    bits = [lax.rem(seq // (1 << b), 2) for b in range(nb)]
    mates = [seq + (1 - 2 * bits[b]) * (1 << b) for b in range(nb)]

    barrier = pltpu.get_barrier_semaphore()
    for b in range(nb):
        pl.semaphore_signal(barrier, inc=1, device_id={"seq": mates[b]})
    for j in range(1, n_dp):
        pl.semaphore_signal(barrier, inc=1, device_id={"dp": lax.rem(dp + j, n_dp)})
    pl.semaphore_wait(barrier, nb + n_dp - 1)

    def cols(c):
        return pl.ds(pl.multiple_of(c * HEAD_DIM, HEAD_DIM), HEAD_DIM)

    def route(c):
        t = lax.rem(c, 4) // 3
        pick = lambda a, l: [a[0] + t * (a[1] - a[0]), a[1] + t * (a[0] - a[1])] + l
        return pick(bits, bits[2:]), pick(mates, mates[2:])

    def size(s):
        return kp_rows >> (s + 1)

    def rows_at(off, s):
        return pl.ds(pl.multiple_of(off, size(s)), size(s))

    def keep(c, s):
        bit, _ = route(c)
        return rows_at(sum(bit[i] * size(i) for i in range(s + 1)), s)

    def give(c, s):
        bit, _ = route(c)
        return rows_at(sum(bit[i] * size(i) for i in range(s)) + (1 - bit[s]) * size(s), s)

    def landing(s):
        return pl.ds(kp_rows - (kp_rows >> s), size(s))

    def copy(kind, s, c, src, dst):
        slot = lax.rem(c, slots)
        return pltpu.make_async_remote_copy(
            src_ref=src, dst_ref=dst,
            send_sem=s_sem.at[kind, s, slot],
            recv_sem=r_sem.at[kind, s, slot],
            device_id={"seq": route(c)[1][s]},
        )

    def kv_copies(c, s):
        slot = lax.rem(c, slots)
        return [
            copy(0, s, c, acc_k.at[slot, give(c, s)], arr_k.at[c, landing(s)]),
            copy(1, s, c, snd_v.at[slot, give(c, s)], arr_v.at[c, landing(s)]),
        ]

    def d_copies(c, s):
        slot = lax.rem(c, slots)
        return [copy(3, s, c, snd_d.at[slot, :, give(c, s)], arr_d.at[c, :, landing(s)])]

    def gather_copies(kind, buf, c, s):
        ref = buf.at[c, :, keep(c, s)]
        return [copy(kind, s, c, ref, ref)]

    def start(copies):
        for one in copies:
            one.start()

    def wait(copies):
        for one in copies:
            one.wait()

    def send_kv(c, s):
        slot = lax.rem(c, slots)
        snd_v[slot, give(c, s)] = acc_v[slot, give(c, s)].astype(bf)
        start(kv_copies(c, s))

    def send_d(c, s):
        slot = lax.rem(c, slots)
        snd_d[slot, :, give(c, s)] = acc_d[slot, :, give(c, s)].astype(bf)
        start(d_copies(c, s))

    def stage_a(c):
        slot = lax.rem(c, slots)
        acc_k[slot] = dot(pk_ref[...], k_ref[:, cols(c)])
        acc_v[slot] = dot(pv_ref[...], v_ref[:, cols(c)])
        send_kv(c, 0)

    def sum_kv(s, c):
        slot = lax.rem(c, slots)
        wait(kv_copies(c, s))
        rows = keep(c, s)
        kt = acc_k[slot, rows] + arr_k[c, landing(s)]
        vt = acc_v[slot, rows] + arr_v[c, landing(s)].astype(jnp.float32)
        if s < nb - 1:
            acc_k[slot, rows] = kt
            acc_v[slot, rows] = vt
            send_kv(c, s + 1)
        else:
            full[c, 0, rows] = kt.astype(bf)
            full[c, 1, rows] = vt.astype(bf)
            start(gather_copies(2, full, c, s))

    def sum_d(s, c):
        slot = lax.rem(c, slots)
        wait(d_copies(c, s))
        rows = keep(c, s)
        total = acc_d[slot, :, rows] + arr_d[c, :, landing(s)].astype(jnp.float32)
        if s < nb - 1:
            acc_d[slot, :, rows] = total
            send_d(c, s + 1)
        else:
            full_d[c, :, rows] = total.astype(bf)
            start(gather_copies(4, full_d, c, s))

    def gather(kind, buf, s, c):
        wait(gather_copies(kind, buf, c, s))
        start(gather_copies(kind, buf, c, s - 1))

    def stage_e(c):
        slot = lax.rem(c, slots)
        wait(gather_copies(2, full, c, 0))
        kp = full[c, 0]
        vp = full[c, 1]
        kpt = kp.astype(jnp.float32).T.astype(bf)
        n_pos = q_ref.shape[0]
        step = min(256, n_pos)
        dk = jnp.zeros((kp_rows, HEAD_DIM), jnp.float32)
        dv = jnp.zeros((kp_rows, HEAD_DIM), jnp.float32)
        for p in range(0, n_pos, step):
            qb = q_ref[pl.ds(p, step), cols(c)]
            gb = g_ref[pl.ds(p, step), cols(c)]
            scores = dot_nt(kp, qb) * scale
            e = jnp.exp(scores - jnp.max(scores, axis=0, keepdims=True))
            probs = e * (1.0 / jnp.sum(e, axis=0, keepdims=True))
            dv += dot(probs.astype(bf), gb)
            gp = dot_nt(vp, gb)
            delta = jnp.sum(probs * gp, axis=0, keepdims=True)
            gs = (probs * (gp - delta) * scale).astype(bf)
            dk += dot(gs, qb)
            gq_ref[pl.ds(p, step), cols(c)] = dot(kpt, gs).T.astype(bf)
        acc_d[slot, 0] = dk
        acc_d[slot, 1] = dv
        send_d(c, 0)

    def stage_i(c):
        wait(gather_copies(4, full_d, c, 0))
        dkp = full_d[c, 0]
        dvp = full_d[c, 1]
        gk_ref[:, cols(c)] = dot(pkt_ref[...], dkp).astype(bf)
        gv_ref[:, cols(c)] = dot(pvt_ref[...], dvp).astype(bf)
        term[0] += dot_nt(dkp, k_ref[:, cols(c)])
        term[1] += dot_nt(dvp, v_ref[:, cols(c)])

    term[...] = jnp.zeros_like(term)

    def turn():
        pkt_ref[...] = pk_ref[...].astype(jnp.float32).T.astype(bf)
        pvt_ref[...] = pv_ref[...].astype(jnp.float32).T.astype(bf)

    stages = [stage_a]
    stages += [functools.partial(sum_kv, s) for s in range(nb)]
    stages += [functools.partial(gather, 2, full, s) for s in range(nb - 1, 0, -1)]
    stages += [stage_e]
    stages += [functools.partial(sum_d, s) for s in range(nb)]
    stages += [functools.partial(gather, 4, full_d, s) for s in range(nb - 1, 0, -1)]
    stages += [stage_i]
    starts, at = [], 0
    for n in range(len(stages)):
        if n in (1, 2 * nb, 2 * nb + 1, 4 * nb):
            at += 1
        at += n > 0
        starts.append(at)

    def iteration(i, _):
        pl.when(i == 1)(turn)
        for at, stage in zip(starts, stages):
            pl.when((i >= at) & (i < at + n_chunks))(functools.partial(stage, i - at))
        return 0

    lax.fori_loop(0, n_chunks + starts[-1], iteration, 0)

    snd_t[...] = term[...].astype(bf)
    copies = []
    for j in range(1, n_dp):
        to = lax.rem(dp + j, n_dp)
        rows = pl.ds(pl.multiple_of(to * t_rows, t_rows), t_rows)
        copies.append(
            pltpu.make_async_remote_copy(
                src_ref=snd_t.at[:, rows], dst_ref=arr_t.at[j - 1],
                send_sem=s_dp.at[j - 1], recv_sem=r_dp.at[j - 1],
                device_id={"dp": to},
            )
        )
    start(copies)
    wait(copies)
    total = term[:, pl.ds(pl.multiple_of(dp * t_rows, t_rows), t_rows)]
    for j in range(1, n_dp):
        total += arr_t[j - 1].astype(jnp.float32)
    sk_ref[...] = total[0].astype(bf)
    sv_ref[...] = total[1].astype(bf)


def body(n_seq, n_dp, query, key, value, grad_ctx, proj_key, proj_value):
    _, n_pos, hd = query.shape
    kp_rows = proj_key.shape[0]
    n_chunks = hd // HEAD_DIM
    nb = n_bits(n_seq)
    slots = n_slots(n_seq)
    t_rows = kp_rows // n_dp
    w = HEAD_DIM
    f32, bf = jnp.float32, jnp.bfloat16
    dma = pltpu.SemaphoreType.DMA
    vmem = pl.BlockSpec(memory_space=pltpu.VMEM)
    wide = jax.ShapeDtypeStruct((n_pos, hd), bf)
    tall = jax.ShapeDtypeStruct((t_rows, n_pos), bf)
    out = pl.pallas_call(
        functools.partial(kernel, n_seq, n_dp),
        out_shape=(wide, wide, wide, tall, tall),
        in_specs=[vmem] * 6,
        out_specs=(vmem,) * 5,
        scratch_shapes=[
            pltpu.VMEM((slots, kp_rows, w), f32),
            pltpu.VMEM((slots, kp_rows, w), f32),
            pltpu.VMEM((slots, kp_rows, w), bf),
            pltpu.VMEM((n_chunks, kp_rows, w), f32),
            pltpu.VMEM((n_chunks, kp_rows, w), bf),
            pltpu.VMEM((n_chunks, 2, kp_rows, w), bf),
            pltpu.VMEM((slots, 2, kp_rows, w), f32),
            pltpu.VMEM((slots, 2, kp_rows, w), bf),
            pltpu.VMEM((n_chunks, 2, kp_rows, w), bf),
            pltpu.VMEM((n_chunks, 2, kp_rows, w), bf),
            pltpu.VMEM((2, kp_rows, n_pos), f32),
            pltpu.VMEM((2, kp_rows, n_pos), bf),
            pltpu.VMEM((n_dp - 1, 2, t_rows, n_pos), bf),
            pltpu.VMEM((n_pos, kp_rows), bf),
            pltpu.VMEM((n_pos, kp_rows), bf),
            dma((5, nb, slots)),
            dma((5, nb, slots)),
            dma((n_dp - 1,)),
            dma((n_dp - 1,)),
        ],
        compiler_params=pltpu.CompilerParams(
            collective_id=0, has_side_effects=True, vmem_limit_bytes=60 * 2**20
        ),
    )(
        query[0], key[0], value[0], grad_ctx[0],
        proj_key, proj_value,
    )
    gq, gk, gv, sk, sv = out
    return gq[None], gk[None], gv[None], sk, sv


def solution(mesh):
    return jax.shard_map(
        functools.partial(body, mesh.shape["seq"], mesh.shape["dp"]),
        mesh=mesh,
        in_specs=(
            P("dp", "seq", None),
            P("dp", "seq", None),
            P("dp", "seq", None),
            P("dp", "seq", None),
            P(None, "seq"),
            P(None, "seq"),
        ),
        out_specs=(
            P("dp", "seq", None),
            P("dp", "seq", None),
            P("dp", "seq", None),
            P("dp", "seq"),
            P("dp", "seq"),
        ),
        check_vma=False,
    )
```
